1024 devices in a mesh: wide: 16 (over x, z_hi, core), narrow: 64 (over y, z_lo).
Axes of the slice: x: 4, y: 4, z: 32 (z_hi: 2, z_lo: 16; z = z_hi * 16 + z_lo), core: 2. Of those that a mesh axis runs over, the one named last changes fastest.
Arguments:
- inputs: bfloat16 [131072, 4096], P(('wide', 'narrow')), may hold values from -6 to 6
- weight_codes: bfloat16 [4096, 512], P('wide'), may hold values from -127 to 127
- code_scales: float32 [4096, 2], P('wide'), may hold values from 0.00010625 to 0.000425
- key_cotangent: bfloat16 [131072, 512], P(('wide', 'narrow')), may hold values from -6 to 6
Outputs:
- keys: bfloat16 [131072, 512], P(('wide', 'narrow'))
- input_grad: bfloat16 [131072, 4096], P(('wide', 'narrow'))
- weight_grad: float32 [4096, 512], P(('wide', 'narrow'))
The draws below stay inside these ranges and needn't reach their ends.
All inputs are finite; a program needn't handle non-finite values.
Results may differ from the reference program's by a relative error of at most 0.015.
Values may be sent and summed in bfloat16 or wider, within the bound.
No kernel may reach another device: no remote copies, remote signals or barrier semaphores. Data moves between devices by JAX's collectives and lax.ppermute only.
A program may use at most 64 MiB of HBM per device.

```python
import math
import jax
import jax.numpy as jnp
from jax import lax

D = 4096
KW = 512
QBLOCK = 256
TOK_DEV = 128
TOKENS = 131072


def level_of(key, extent, split, smallest, largest):
    gain = 1.0
    for axis_at, shards_of in split:
        draws = jax.random.uniform(jax.random.fold_in(jax.random.fold_in(key, 6), axis_at), (shards_of,), jnp.float32, smallest / len(split), largest / len(split))
        gain = gain * jnp.repeat(jnp.exp(draws), extent[axis_at] // shards_of).reshape((-1,) + (1,) * (len(extent) - 1 - axis_at))
    return gain


def noise(rng, shape, deviation, reach, cuts=(), kind=jnp.bfloat16):
    result = jax.random.normal(rng, shape, jnp.float32) * deviation
    if len(cuts) > 0:
        result = level_of(rng, shape, cuts, -0.22, 0.18) * result
    return jnp.clip(result, min=-reach, max=reach).astype(kind)


def setup_inputs(seed: int = 0) -> dict:
    key_of = jax.random.split(jax.random.key(seed), 5)
    inputs = noise(key_of[0], (TOKENS, D), 1.0, 6.0, ((0, 1024),))
    weight_codes = jnp.clip(jax.random.uniform(key_of[1], (D, KW), jnp.float32, -127.0, 127.0) * level_of(key_of[1], (D, KW), ((0, 16),), -0.4, 0.0), -127.0, 127.0).astype(jnp.bfloat16)
    code_scales = jnp.clip(jnp.exp(math.log(0.000425) - 1.3862944 * jax.random.uniform(key_of[2], (D, KW // QBLOCK), jnp.float32) ** level_of(key_of[2], (D, KW // QBLOCK), ((0, 16),), -0.2, 0.2)), 0.00010625, 0.000425)
    key_cotangent = noise(key_of[3], (TOKENS, KW), 1.0, 6.0, ((0, 1024),))
    return dict(inputs=inputs, weight_codes=weight_codes, code_scales=code_scales, key_cotangent=key_cotangent)


def dequantize(codes, scales):
    rows = codes.shape[0]
    blocks = codes.astype(jnp.float32).reshape(rows, scales.shape[1], -1) * scales[:, :, None]
    return blocks.reshape(rows, codes.shape[1]).astype(jnp.bfloat16)


def reference(inputs, weight_codes, code_scales, key_cotangent):
    weight = dequantize(weight_codes, code_scales)
    keys = jnp.dot(inputs, weight, preferred_element_type=jnp.float32).astype(jnp.bfloat16)
    input_grad = jnp.dot(key_cotangent, weight.T, preferred_element_type=jnp.float32).astype(jnp.bfloat16)
    count = inputs.shape[0] // TOK_DEV
    blocks_in = inputs.reshape(count, TOK_DEV, D)
    blocks_co = key_cotangent.reshape(count, TOK_DEV, KW)

    def step(total, pair):
        term = jnp.dot(pair[0].T, pair[1], preferred_element_type=jnp.float32).astype(jnp.bfloat16)
        return total + term.astype(jnp.float32), None

    weight_grad, _ = lax.scan(step, jnp.zeros((D, KW), jnp.float32), (blocks_in, blocks_co))
    return keys, input_grad, weight_grad
```

```python
import functools

import jax
import jax.numpy as jnp
from jax import lax
from jax.experimental import pallas as pl
from jax.experimental.pallas import tpu as pltpu
from jax.sharding import PartitionSpec as P

BOTH = ("wide", "narrow")
BF16, F32 = jnp.bfloat16, jnp.float32
VMEM_LIMIT = 48 * 1024 * 1024


def flat(x, y, z, c):
    x, y, z = x % 4, y % 4, z % 32
    return ((x * 2 + z // 16) * 2 + c) * 64 + y * 16 + z % 16


def pairs(move):
    return [
        (flat(x, y, z, c), flat(*move(x, y, z, c)))
        for x in range(4)
        for y in range(4)
        for z in range(32)
        for c in range(2)
    ]


def first_axis(d):
    return pairs(lambda x, y, z, c: (x + d, y, z, c) if c == 0 else (x, y + d, z, c))


def second_axis(d):
    return pairs(lambda x, y, z, c: (x, y + d, z, c) if c == 0 else (x + d, y, z, c))


def core_swap():
    return pairs(lambda x, y, z, c: (x, y, z, 1 - c))


def half_swap():
    return pairs(lambda x, y, z, c: (x, y, z + 8 if z % 16 >= 8 else z - 8, c))


def z_groups():
    return [
        [flat(x, y, z, c) for z in range(32)] for x in range(4) for y in range(4) for c in range(2)
    ]


def coords():
    w, n = lax.axis_index("wide"), lax.axis_index("narrow")
    return lax.div(w, 4), lax.div(n, 16), lax.rem(lax.div(w, 2), 2), lax.rem(w, 2)


def up(v, d):
    return lax.rem(v + d, 4)


def down(v, d):
    return lax.rem(v + 4 - d, 4)


def rows_at(i, size):
    return pl.ds(pl.multiple_of(i * size, size), size)


def call(body, outs, ins, scratch=(), flops=0):
    moved = sum(a.size * a.dtype.itemsize for a in (*ins, *outs))
    return pl.pallas_call(
        body,
        out_shape=outs,
        in_specs=[pl.BlockSpec(memory_space=pltpu.VMEM)] * len(ins),
        out_specs=[pl.BlockSpec(memory_space=pltpu.VMEM)] * len(outs),
        scratch_shapes=scratch,
        compiler_params=pltpu.CompilerParams(vmem_limit_bytes=VMEM_LIMIT),
        cost_estimate=pl.CostEstimate(flops=flops, bytes_accessed=moved, transcendentals=0),
    )(*ins)


def term_body(other, x_ref, k_ref, out_ref):
    _, _, _, c = coords()
    cc = 1 - c if other else c
    for b in range(8):
        block = x_ref[:, rows_at(2 * b + cc, 256)]
        out_ref[b * 256 : (b + 1) * 256, :] = lax.dot_general(
            block, k_ref[...], (((0,), (0,)), ((), ())), preferred_element_type=F32
        ).astype(out_ref.dtype)


def split_first_body(keep_ref, got_ref, mine_ref, *out_refs):
    x, y, _, c = coords()
    for d in range(4):
        ref = mine_ref if d == 0 else out_refs[d - 1]
        for j in range(4):
            to_x = jnp.where(c == 0, up(x, d), j)
            to_y = jnp.where(c == 0, j, up(y, d))
            for h in range(2):
                rows = rows_at((to_x * 2 + h) * 4 + to_y, 64)
                total = keep_ref[rows, :].astype(F32) + got_ref[rows, :].astype(F32)
                ref[j, h] = total.astype(ref.dtype)


def split_second_body(own_ref, a_ref, b_ref, c_ref, mine_ref, *out_refs):
    x, y, _, c = coords()
    me = jnp.where(c == 0, y, x)
    for e in range(4):
        ref = mine_ref if e == 0 else out_refs[e - 1]
        j = up(me, e)
        total = own_ref[j] + a_ref[j].astype(F32) + b_ref[j].astype(F32) + c_ref[j].astype(F32)
        ref[...] = total.astype(ref.dtype)


def project_body(x_ref, k_ref, *refs):
    pieces, (keys_ref, grad_ref, weight_ref) = refs[:8], refs[8:]
    x, y, zh, c = coords()
    for s in range(2):
        core = c if s == 0 else 1 - c
        for e in range(4):
            for d in range(4):
                at_x = jnp.where(core == 0, down(x, d), down(x, e))
                at_y = jnp.where(core == 0, down(y, e), down(y, d))
                for r in range(2):
                    h = zh if r == 0 else 1 - zh
                    rows = rows_at(((at_x * 2 + h) * 2 + core) * 4 + at_y, 64)
                    weight_ref[rows, :] = pieces[s * 4 + e][d, r]
    keys_ref[...] = jnp.dot(x_ref[...], weight_ref[...], preferred_element_type=F32).astype(BF16)
    for b in range(8):
        rows = slice(b * 512, (b + 1) * 512)
        grad_ref[:, rows] = lax.dot_general(
            k_ref[...], weight_ref[rows, :], (((1,), (1,)), ((), ())), preferred_element_type=F32
        ).astype(BF16)


def dequantize(codes, scales):
    rows = codes.shape[0]
    blocks = codes.astype(F32).reshape(rows, scales.shape[1], -1) * scales[:, :, None]
    return blocks.reshape(rows, codes.shape[1]).astype(BF16)


def shape(dims, dtype):
    return jax.ShapeDtypeStruct(dims, dtype)


def shards(inputs, weight_codes, code_scales, key_cotangent):
    y = coords()[1]
    swap = core_swap()

    weight = dequantize(weight_codes, code_scales)
    quarter = lax.dynamic_slice(weight, (y * 64, 0), (64, 512))
    other = lax.ppermute(quarter, BOTH, half_swap())

    flops = 2 * 128 * 2048 * 512
    sent = call(
        functools.partial(term_body, True),
        [shape((2048, 512), BF16)],
        (inputs, key_cotangent),
        flops=flops,
    )[0]
    got = lax.ppermute(sent, BOTH, swap)
    keep = call(
        functools.partial(term_body, False),
        [shape((2048, 512), F32)],
        (inputs, key_cotangent),
        flops=flops,
    )[0]

    base = jnp.stack([quarter, other])
    line = jnp.stack([base] + [lax.ppermute(base, BOTH, first_axis(d)) for d in (1, 2, 3)])

    chunk = (4, 2, 64, 512)
    mine, *outs = call(
        split_first_body, [shape(chunk, F32)] + [shape(chunk, BF16)] * 3, (keep, got)
    )
    ins = [lax.ppermute(o, BOTH, first_axis(d)) for d, o in zip((1, 2, 3), outs)]

    plane = [line] + [lax.ppermute(line, BOTH, second_axis(d)) for d in (1, 2, 3)]

    chunk = (2, 64, 512)
    mine, *outs = call(
        split_second_body, [shape(chunk, F32)] + [shape(chunk, BF16)] * 3, (mine, *ins)
    )
    ins = [lax.ppermute(o, BOTH, second_axis(d)) for d, o in zip((1, 2, 3), outs)]
    swapped = [lax.ppermute(p, BOTH, swap) for p in plane]

    column = mine + sum(i.astype(F32) for i in ins)
    column = column.astype(BF16).reshape(32, 4, 4, 128).reshape(32, 16, 128)
    column = lax.all_to_all(column, BOTH, 0, 0, tiled=True, axis_index_groups=z_groups())
    weight_grad = jnp.sum(column.astype(F32), axis=0).reshape(4, 512)

    keys, input_grad = call(
        project_body,
        [shape((128, 512), BF16), shape((128, 4096), BF16)],
        (inputs, key_cotangent, *plane, *swapped),
        scratch=[pltpu.VMEM((4096, 512), BF16)],
        flops=4 * 128 * 4096 * 512,
    )
    return keys, input_grad, weight_grad


def solution(mesh):
    return jax.shard_map(
        shards,
        mesh=mesh,
        in_specs=(P(BOTH, None), P("wide", None), P("wide", None), P(BOTH, None)),
        out_specs=(P(BOTH, None), P(BOTH, None), P(BOTH, None)),
        check_vma=False,
    )
```

```python
import functools

import jax
import jax.numpy as jnp
from jax import lax
from jax.experimental import pallas as pl
from jax.experimental.pallas import tpu as pltpu
from jax.sharding import PartitionSpec as P

BOTH = ("wide", "narrow")
BF16, F32 = jnp.bfloat16, jnp.float32
VMEM_LIMIT = 48 * 1024 * 1024


def flat(x, y, z, c):
    x, y, z = x % 4, y % 4, z % 32
    return ((x * 2 + z // 16) * 2 + c) * 64 + y * 16 + z % 16


def pairs(move):
    return [
        (flat(x, y, z, c), flat(*move(x, y, z, c)))
        for x in range(4)
        for y in range(4)
        for z in range(32)
        for c in range(2)
    ]


def first_axis(d):
    return pairs(lambda x, y, z, c: (x + d, y, z, c) if c == 0 else (x, y + d, z, c))


def second_axis(d):
    return pairs(lambda x, y, z, c: (x, y + d, z, c) if c == 0 else (x + d, y, z, c))


def core_swap():
    return pairs(lambda x, y, z, c: (x, y, z, 1 - c))


def half_swap():
    return pairs(lambda x, y, z, c: (x, y, z + 8 if z % 16 >= 8 else z - 8, c))


def z_groups():
    return [
        [flat(x, y, z, c) for z in range(32)] for x in range(4) for y in range(4) for c in range(2)
    ]


def coords():
    w, n = lax.axis_index("wide"), lax.axis_index("narrow")
    return lax.div(w, 4), lax.div(n, 16), lax.rem(lax.div(w, 2), 2), lax.rem(w, 2)


def up(v, d):
    return lax.rem(v + d, 4)


def down(v, d):
    return lax.rem(v + 4 - d, 4)


def rows_at(i, size):
    return pl.ds(pl.multiple_of(i * size, size), size)


def call(body, outs, ins, scratch=(), flops=0):
    moved = sum(a.size * a.dtype.itemsize for a in (*ins, *outs))
    return pl.pallas_call(
        body,
        out_shape=outs,
        in_specs=[pl.BlockSpec(memory_space=pltpu.VMEM)] * len(ins),
        out_specs=[pl.BlockSpec(memory_space=pltpu.VMEM)] * len(outs),
        scratch_shapes=scratch,
        compiler_params=pltpu.CompilerParams(vmem_limit_bytes=VMEM_LIMIT),
        cost_estimate=pl.CostEstimate(flops=flops, bytes_accessed=moved, transcendentals=0),
    )(*ins)


def term_body(other, x_ref, k_ref, out_ref):
    _, _, _, c = coords()
    cc = 1 - c if other else c
    for b in range(8):
        block = x_ref[:, rows_at(2 * b + cc, 256)]
        out_ref[b * 256 : (b + 1) * 256, :] = lax.dot_general(
            block, k_ref[...], (((0,), (0,)), ((), ())), preferred_element_type=F32
        ).astype(out_ref.dtype)


def split_first_body(keep_ref, got_ref, mine_ref, *out_refs):
    x, y, _, c = coords()
    for d in range(4):
        ref = mine_ref if d == 0 else out_refs[d - 1]
        for j in range(4):
            to_x = jnp.where(c == 0, up(x, d), j)
            to_y = jnp.where(c == 0, j, up(y, d))
            for h in range(2):
                rows = rows_at((to_x * 2 + h) * 4 + to_y, 64)
                total = keep_ref[rows, :].astype(F32) + got_ref[rows, :].astype(F32)
                ref[j, h] = total.astype(ref.dtype)


def split_second_body(own_ref, a_ref, b_ref, c_ref, w_ref, v_ref, mine_ref, *out_refs):
    x, y, _, c = coords()
    me = jnp.where(c == 0, y, x)
    for e in range(4):
        j = up(me, e)
        total = own_ref[j] + a_ref[j].astype(F32) + b_ref[j].astype(F32) + c_ref[j].astype(F32)
        if e == 0:
            mine_ref[...] = total
        else:
            out_refs[e - 1][0] = total.astype(BF16)
            out_refs[e - 1][1, 0] = w_ref[...]
            out_refs[e - 1][1, 1] = v_ref[...]


def project_body(x_ref, k_ref, own_ref, got_ref, keys_ref, grad_ref, weight_ref):
    x, y, zh, c = coords()
    for s in range(2):
        core = c if s == 0 else 1 - c
        ref = own_ref if s == 0 else got_ref
        for e in range(4):
            for d in range(4):
                at_x = jnp.where(core == 0, down(x, e), down(x, d))
                at_y = jnp.where(core == 0, down(y, d), down(y, e))
                for r in range(2):
                    h = zh if r == 0 else 1 - zh
                    rows = rows_at(((at_x * 2 + h) * 2 + core) * 4 + at_y, 64)
                    weight_ref[rows, :] = ref[e, d, r]
    keys_ref[...] = jnp.dot(x_ref[...], weight_ref[...], preferred_element_type=F32).astype(BF16)
    for b in range(8):
        rows = slice(b * 512, (b + 1) * 512)
        grad_ref[:, rows] = lax.dot_general(
            k_ref[...], weight_ref[rows, :], (((1,), (1,)), ((), ())), preferred_element_type=F32
        ).astype(BF16)


def dequantize(codes, scales):
    rows = codes.shape[0]
    blocks = codes.astype(F32).reshape(rows, scales.shape[1], -1) * scales[:, :, None]
    return blocks.reshape(rows, codes.shape[1]).astype(BF16)


def shape(dims, dtype):
    return jax.ShapeDtypeStruct(dims, dtype)


def shards(inputs, weight_codes, code_scales, key_cotangent):
    y = coords()[1]

    quarter = dequantize(
        lax.dynamic_slice(weight_codes, (y * 64, 0), (64, 512)),
        lax.dynamic_slice(code_scales, (y * 64, 0), (64, 2)),
    )
    other = lax.ppermute(quarter, BOTH, half_swap())

    flops = 2 * 128 * 2048 * 512
    sent = call(
        functools.partial(term_body, True),
        [shape((2048, 512), BF16)],
        (inputs, key_cotangent),
        flops=flops,
    )[0]
    got = lax.ppermute(sent, BOTH, core_swap())
    keep = call(
        functools.partial(term_body, False),
        [shape((2048, 512), F32)],
        (inputs, key_cotangent),
        flops=flops,
    )[0]

    chunk = (4, 2, 64, 512)
    mine, *outs = call(
        split_first_body, [shape(chunk, F32)] + [shape(chunk, BF16)] * 3, (keep, got)
    )
    ins = [lax.ppermute(o, BOTH, first_axis(d)) for d, o in zip((1, 2, 3), outs)]

    mine, *outs = call(
        split_second_body,
        [shape((2, 64, 512), F32)] + [shape((2, 2, 64, 512), BF16)] * 3,
        (mine, *ins, quarter, other),
    )
    ins = [lax.ppermute(o, BOTH, second_axis(d)) for d, o in zip((1, 2, 3), outs)]

    line = jnp.stack([jnp.stack([quarter, other])] + [i[1] for i in ins])
    plane = jnp.stack([line] + [lax.ppermute(line, BOTH, first_axis(d)) for d in (1, 2, 3)])
    swapped = lax.ppermute(plane, BOTH, core_swap())

    column = mine + sum(i[0].astype(F32) for i in ins)
    column = column.astype(BF16).reshape(32, 4, 4, 128).reshape(32, 16, 128)
    column = lax.all_to_all(column, BOTH, 0, 0, tiled=True, axis_index_groups=z_groups())
    weight_grad = jnp.sum(column.astype(F32), axis=0).reshape(4, 512)

    keys, input_grad = call(
        project_body,
        [shape((128, 512), BF16), shape((128, 4096), BF16)],
        (inputs, key_cotangent, plane, swapped),
        scratch=[pltpu.VMEM((4096, 512), BF16)],
        flops=4 * 128 * 4096 * 512,
    )
    return keys, input_grad, weight_grad


def solution(mesh):
    return jax.shard_map(
        shards,
        mesh=mesh,
        in_specs=(P(BOTH, None), P("wide", None), P("wide", None), P(BOTH, None)),
        out_specs=(P(BOTH, None), P(BOTH, None), P(BOTH, None)),
        check_vma=False,
    )
```

```python
import functools

import jax
import jax.numpy as jnp
from jax import lax
from jax.experimental import pallas as pl
from jax.experimental.pallas import tpu as pltpu
from jax.sharding import PartitionSpec as P

BOTH = ("wide", "narrow")
BF16, F32 = jnp.bfloat16, jnp.float32
VMEM_LIMIT = 48 * 1024 * 1024


def flat(x, y, z, c):
    x, y, z = x % 4, y % 4, z % 32
    return ((x * 2 + z // 16) * 2 + c) * 64 + y * 16 + z % 16


def pairs(move):
    return [
        (flat(x, y, z, c), flat(*move(x, y, z, c)))
        for x in range(4)
        for y in range(4)
        for z in range(32)
        for c in range(2)
    ]


def first_axis(d):
    return pairs(lambda x, y, z, c: (x + d, y, z, c) if c == 0 else (x, y + d, z, c))


def second_axis(d):
    return pairs(lambda x, y, z, c: (x, y + d, z, c) if c == 0 else (x + d, y, z, c))


def core_swap():
    return pairs(lambda x, y, z, c: (x, y, z, 1 - c))


def half_swap():
    return pairs(lambda x, y, z, c: (x, y, z + 8 if z % 16 >= 8 else z - 8, c))


def z_groups():
    return [
        [flat(x, y, z, c) for z in range(32)] for x in range(4) for y in range(4) for c in range(2)
    ]


def coords():
    w, n = lax.axis_index("wide"), lax.axis_index("narrow")
    return lax.div(w, 4), lax.div(n, 16), lax.rem(lax.div(w, 2), 2), lax.rem(w, 2)


def up(v, d):
    return lax.rem(v + d, 4)


def down(v, d):
    return lax.rem(v + 4 - d, 4)


def rows_at(i, size):
    return pl.ds(pl.multiple_of(i * size, size), size)


def call(body, outs, ins, scratch=(), flops=0):
    moved = sum(a.size * a.dtype.itemsize for a in (*ins, *outs))
    return pl.pallas_call(
        body,
        out_shape=outs,
        in_specs=[pl.BlockSpec(memory_space=pltpu.VMEM)] * len(ins),
        out_specs=[pl.BlockSpec(memory_space=pltpu.VMEM)] * len(outs),
        scratch_shapes=scratch,
        compiler_params=pltpu.CompilerParams(vmem_limit_bytes=VMEM_LIMIT),
        cost_estimate=pl.CostEstimate(flops=flops, bytes_accessed=moved, transcendentals=0),
    )(*ins)


def term_body(other, x_ref, k_ref, out_ref):
    _, _, _, c = coords()
    cc = 1 - c if other else c
    for b in range(8):
        block = x_ref[:, rows_at(2 * b + cc, 256)]
        out_ref[b * 256 : (b + 1) * 256, :] = lax.dot_general(
            block, k_ref[...], (((0,), (0,)), ((), ())), preferred_element_type=F32
        ).astype(out_ref.dtype)


def split_first_body(keep_ref, got_ref, mine_ref, *out_refs):
    x, y, _, c = coords()
    for d in range(4):
        ref = mine_ref if d == 0 else out_refs[d - 1]
        for j in range(4):
            to_x = jnp.where(c == 0, up(x, d), j)
            to_y = jnp.where(c == 0, j, up(y, d))
            for h in range(2):
                rows = rows_at((to_x * 2 + h) * 4 + to_y, 64)
                total = keep_ref[rows, :].astype(F32) + got_ref[rows, :].astype(F32)
                ref[j, h] = total.astype(ref.dtype)


def split_second_body(own_ref, a_ref, b_ref, c_ref, w_ref, v_ref, mine_ref, *out_refs):
    x, y, _, c = coords()
    me = jnp.where(c == 0, y, x)
    for e in range(4):
        j = up(me, e)
        total = own_ref[j] + a_ref[j].astype(F32) + b_ref[j].astype(F32) + c_ref[j].astype(F32)
        if e == 0:
            mine_ref[...] = total
        else:
            out_refs[e - 1][0] = total.astype(BF16)
            out_refs[e - 1][1, 0] = w_ref[...]
            out_refs[e - 1][1, 1] = v_ref[...]


def project_body(x_ref, k_ref, *refs):
    pieces, (keys_ref, grad_ref, weight_ref) = refs[:8], refs[8:]
    x, y, zh, c = coords()
    for s in range(2):
        core = c if s == 0 else 1 - c
        for e in range(4):
            for d in range(4):
                at_x = jnp.where(core == 0, down(x, e), down(x, d))
                at_y = jnp.where(core == 0, down(y, d), down(y, e))
                for r in range(2):
                    h = zh if r == 0 else 1 - zh
                    rows = rows_at(((at_x * 2 + h) * 2 + core) * 4 + at_y, 64)
                    weight_ref[rows, :] = pieces[s * 4 + e][d, r]
    keys_ref[...] = jnp.dot(x_ref[...], weight_ref[...], preferred_element_type=F32).astype(BF16)
    for b in range(8):
        rows = slice(b * 512, (b + 1) * 512)
        grad_ref[:, rows] = lax.dot_general(
            k_ref[...], weight_ref[rows, :], (((1,), (1,)), ((), ())), preferred_element_type=F32
        ).astype(BF16)


def dequantize(codes, scales):
    rows = codes.shape[0]
    blocks = codes.astype(F32).reshape(rows, scales.shape[1], -1) * scales[:, :, None]
    return blocks.reshape(rows, codes.shape[1]).astype(BF16)


def shape(dims, dtype):
    return jax.ShapeDtypeStruct(dims, dtype)


def shards(inputs, weight_codes, code_scales, key_cotangent):
    y = coords()[1]

    quarter = dequantize(
        lax.dynamic_slice(weight_codes, (y * 64, 0), (64, 512)),
        lax.dynamic_slice(code_scales, (y * 64, 0), (64, 2)),
    )
    other = lax.ppermute(quarter, BOTH, half_swap())

    flops = 2 * 128 * 2048 * 512
    sent = call(
        functools.partial(term_body, True),
        [shape((2048, 512), BF16)],
        (inputs, key_cotangent),
        flops=flops,
    )[0]
    got = lax.ppermute(sent, BOTH, core_swap())
    keep = call(
        functools.partial(term_body, False),
        [shape((2048, 512), F32)],
        (inputs, key_cotangent),
        flops=flops,
    )[0]

    chunk = (4, 2, 64, 512)
    mine, *outs = call(
        split_first_body, [shape(chunk, F32)] + [shape(chunk, BF16)] * 3, (keep, got)
    )
    outs[1], other = lax.optimization_barrier((outs[1], other))
    ins = [lax.ppermute(o, BOTH, first_axis(d)) for d, o in zip((1, 2, 3), outs)]

    mine, *outs = call(
        split_second_body,
        [shape((2, 64, 512), F32)] + [shape((2, 2, 64, 512), BF16)] * 3,
        (mine, *ins, quarter, other),
    )
    ins = [lax.ppermute(o, BOTH, second_axis(d)) for d, o in zip((1, 2, 3), outs)]

    line = jnp.stack([jnp.stack([quarter, other])] + [i[1] for i in ins])
    column = mine + sum(i[0].astype(F32) for i in ins)
    column = column.astype(BF16).reshape(32, 4, 4, 128).reshape(32, 16, 128)
    plane = [line] + [lax.ppermute(line, BOTH, first_axis(d)) for d in (1, 2, 3)]
    swapped = [lax.ppermute(p, BOTH, core_swap()) for p in plane]

    column = lax.all_to_all(column, BOTH, 0, 0, tiled=True, axis_index_groups=z_groups())
    weight_grad = jnp.sum(column.astype(F32), axis=0).reshape(4, 512)

    keys, input_grad = call(
        project_body,
        [shape((128, 512), BF16), shape((128, 4096), BF16)],
        (inputs, key_cotangent, *plane, *swapped),
        scratch=[pltpu.VMEM((4096, 512), BF16)],
        flops=4 * 128 * 4096 * 512,
    )
    return keys, input_grad, weight_grad


def solution(mesh):
    return jax.shard_map(
        shards,
        mesh=mesh,
        in_specs=(P(BOTH, None), P("wide", None), P("wide", None), P(BOTH, None)),
        out_specs=(P(BOTH, None), P(BOTH, None), P(BOTH, None)),
        check_vma=False,
    )
```

```python
import functools

import jax
import jax.numpy as jnp
from jax import lax
from jax.experimental import pallas as pl
from jax.experimental.pallas import tpu as pltpu
from jax.sharding import PartitionSpec as P

BOTH = ("wide", "narrow")
BF16, F32 = jnp.bfloat16, jnp.float32
VMEM_LIMIT = 48 * 1024 * 1024


def flat(x, y, z, c):
    x, y, z = x % 4, y % 4, z % 32
    return ((x * 2 + z // 16) * 2 + c) * 64 + y * 16 + z % 16


def pairs(move):
    return [
        (flat(x, y, z, c), flat(*move(x, y, z, c)))
        for x in range(4)
        for y in range(4)
        for z in range(32)
        for c in range(2)
    ]


def first_axis(d):
    return pairs(lambda x, y, z, c: (x + d, y, z, c) if c == 0 else (x, y + d, z, c))


def second_axis(d):
    return pairs(lambda x, y, z, c: (x, y + d, z, c) if c == 0 else (x + d, y, z, c))


def core_swap():
    return pairs(lambda x, y, z, c: (x, y, z, 1 - c))


def half_swap():
    return pairs(lambda x, y, z, c: (x, y, z + 8 if z % 16 >= 8 else z - 8, c))


def z_groups():
    return [
        [flat(x, y, z, c) for z in range(32)] for x in range(4) for y in range(4) for c in range(2)
    ]


def coords():
    w, n = lax.axis_index("wide"), lax.axis_index("narrow")
    return lax.div(w, 4), lax.div(n, 16), lax.rem(lax.div(w, 2), 2), lax.rem(w, 2)


def up(v, d):
    return lax.rem(v + d, 4)


def down(v, d):
    return lax.rem(v + 4 - d, 4)


def rows_at(i, size):
    return pl.ds(pl.multiple_of(i * size, size), size)


def call(body, outs, ins, scratch=(), flops=0):
    moved = sum(a.size * a.dtype.itemsize for a in (*ins, *outs))
    return pl.pallas_call(
        body,
        out_shape=outs,
        in_specs=[pl.BlockSpec(memory_space=pltpu.VMEM)] * len(ins),
        out_specs=[pl.BlockSpec(memory_space=pltpu.VMEM)] * len(outs),
        scratch_shapes=scratch,
        compiler_params=pltpu.CompilerParams(vmem_limit_bytes=VMEM_LIMIT),
        cost_estimate=pl.CostEstimate(flops=flops, bytes_accessed=moved, transcendentals=0),
    )(*ins)


def term_body(other, x_ref, k_ref, out_ref):
    _, _, _, c = coords()
    cc = 1 - c if other else c
    for b in range(8):
        block = x_ref[:, rows_at(2 * b + cc, 256)]
        out_ref[b * 256 : (b + 1) * 256, :] = lax.dot_general(
            block, k_ref[...], (((0,), (0,)), ((), ())), preferred_element_type=F32
        ).astype(out_ref.dtype)


def split_first_body(keep_ref, got_ref, mine_ref, *out_refs):
    x, y, _, c = coords()
    for d in range(4):
        ref = mine_ref if d == 0 else out_refs[d - 1]
        for j in range(4):
            to_x = jnp.where(c == 0, up(x, d), j)
            to_y = jnp.where(c == 0, j, up(y, d))
            for h in range(2):
                rows = rows_at((to_x * 2 + h) * 4 + to_y, 64)
                total = keep_ref[rows, :].astype(F32) + got_ref[rows, :].astype(F32)
                ref[j, h] = total.astype(ref.dtype)


def split_second_body(own_ref, a_ref, b_ref, c_ref, mine_ref, *out_refs):
    x, y, _, c = coords()
    me = jnp.where(c == 0, y, x)
    for e in range(4):
        ref = mine_ref if e == 0 else out_refs[e - 1]
        j = up(me, e)
        total = own_ref[j] + a_ref[j].astype(F32) + b_ref[j].astype(F32) + c_ref[j].astype(F32)
        ref[...] = total.astype(ref.dtype)


def project_body(x_ref, k_ref, *refs):
    pieces, (keys_ref, grad_ref, weight_ref) = refs[:8], refs[8:]
    x, y, zh, c = coords()
    for s in range(2):
        core = c if s == 0 else 1 - c
        for e in range(4):
            for d in range(4):
                at_x = jnp.where(core == 0, down(x, e), down(x, d))
                at_y = jnp.where(core == 0, down(y, d), down(y, e))
                for r in range(2):
                    h = zh if r == 0 else 1 - zh
                    rows = rows_at(((at_x * 2 + h) * 2 + core) * 4 + at_y, 64)
                    weight_ref[rows, :] = pieces[s * 4 + e][d, r]
    keys_ref[...] = jnp.dot(x_ref[...], weight_ref[...], preferred_element_type=F32).astype(BF16)
    for b in range(8):
        rows = slice(b * 512, (b + 1) * 512)
        grad_ref[:, rows] = lax.dot_general(
            k_ref[...], weight_ref[rows, :], (((1,), (1,)), ((), ())), preferred_element_type=F32
        ).astype(BF16)


def dequantize(codes, scales):
    rows = codes.shape[0]
    blocks = codes.astype(F32).reshape(rows, scales.shape[1], -1) * scales[:, :, None]
    return blocks.reshape(rows, codes.shape[1]).astype(BF16)


def shape(dims, dtype):
    return jax.ShapeDtypeStruct(dims, dtype)


def shards(inputs, weight_codes, code_scales, key_cotangent):
    y = coords()[1]

    quarter = dequantize(
        lax.dynamic_slice(weight_codes, (y * 64, 0), (64, 512)),
        lax.dynamic_slice(code_scales, (y * 64, 0), (64, 2)),
    )
    other = lax.ppermute(quarter, BOTH, half_swap())

    flops = 2 * 128 * 2048 * 512
    sent = call(
        functools.partial(term_body, True),
        [shape((2048, 512), BF16)],
        (inputs, key_cotangent),
        flops=flops,
    )[0]
    got = lax.ppermute(sent, BOTH, core_swap())
    keep = call(
        functools.partial(term_body, False),
        [shape((2048, 512), BF16)],
        (inputs, key_cotangent),
        flops=flops,
    )[0]

    chunk = (4, 2, 64, 512)
    mine, *outs = call(
        split_first_body, [shape(chunk, F32)] + [shape(chunk, BF16)] * 3, (keep, got)
    )
    ins = [lax.ppermute(o, BOTH, first_axis(d)) for d, o in zip((1, 2, 3), outs)]

    mine, *outs = call(
        split_second_body,
        [shape((2, 64, 512), F32)] + [shape((2, 64, 512), BF16)] * 3,
        (mine, *ins),
    )
    ins = [lax.ppermute(o, BOTH, second_axis(d)) for d, o in zip((1, 2, 3), outs)]

    column = mine + sum(i.astype(F32) for i in ins)
    column = column.astype(BF16).reshape(32, 4, 4, 128).reshape(32, 16, 128)
    base = jnp.stack([quarter, other])
    base, column = lax.optimization_barrier((base, column))
    line = jnp.stack([base] + [lax.ppermute(base, BOTH, second_axis(d)) for d in (1, 2, 3)])
    plane = [line] + [lax.ppermute(line, BOTH, first_axis(d)) for d in (1, 2, 3)]
    swapped = [lax.ppermute(p, BOTH, core_swap()) for p in plane]

    column = lax.all_to_all(column, BOTH, 0, 0, tiled=True, axis_index_groups=z_groups())
    weight_grad = jnp.sum(column.astype(F32), axis=0).reshape(4, 512)

    keys, input_grad = call(
        project_body,
        [shape((128, 512), BF16), shape((128, 4096), BF16)],
        (inputs, key_cotangent, *plane, *swapped),
        scratch=[pltpu.VMEM((4096, 512), BF16)],
        flops=4 * 128 * 4096 * 512,
    )
    return keys, input_grad, weight_grad


def solution(mesh):
    return jax.shard_map(
        shards,
        mesh=mesh,
        in_specs=(P(BOTH, None), P("wide", None), P("wide", None), P(BOTH, None)),
        out_specs=(P(BOTH, None), P(BOTH, None), P(BOTH, None)),
        check_vma=False,
    )
```
